32 devices in a mesh: group: 2 (over x), dp: 8 (over z, y), mp: 2 (over core).
Axes of the slice: x: 2, y: 2, z: 4, core: 2. Of those that a mesh axis runs over, the one named last changes fastest.
Arguments:
- input_tiles: bfloat16 [24576, 4096], P(('group', 'dp'), 'mp'), parts along dimension 0, may hold values from -6 to 6
- value_matrix: bfloat16 [4096, 1024], P('mp', 'dp'), may hold values from -0.09375 to 0.09375
- adapter_down_weight: bfloat16 [32, 4096, 32], P(('group', 'dp'), 'mp'), parts along dimension 0, may hold values from -0.09375 to 0.09375
- adapter_up_weight: bfloat16 [32, 32, 1024], P(('group', 'dp'), None, 'mp'), parts along dimension 0, may hold values from -1 to 1
- output_gradient: bfloat16 [24576, 1024], P(('group', 'dp'), 'mp'), parts along dimension 0, may hold values from -3 to 3
- tile_slot_target: int32 [192], P('group'), parts along dimension 0, may hold values from -1 to 95, as said below
- tile_owner_tenant: int32 [192], P('group'), parts along dimension 0, may hold values from 0 to 15, as said below
- tenant_storage_row: int32 [32], P('group'), parts along dimension 0, may hold values from 0 to 15, as said below
Outputs:
- moved_out: bfloat16 [24576, 1024], P(('group', 'dp'), 'mp'), parts along dimension 0
- grad_a: float32 [32, 4096, 32], P(('group', 'dp'), 'mp'), parts along dimension 0
- grad_b: float32 [32, 32, 1024], P(('group', 'dp'), None, 'mp'), parts along dimension 0
The draws below stay inside these ranges and needn't reach their ends.
There are 2 independent parts, one for each index of `group`. The reference program is written for one: setup_inputs(seed, part) draws one part's arguments, and reference() takes and returns one part's arrays. A program takes and returns all parts, laid end to end along the dimension named above; an argument that names none is the same for every part. Nothing has to cross between parts.
Inputs may be any that keep to these rules, and one draw needn't show every extreme that they name: `tile_slot_target`: tile r * 12 + j sits on rank r of dp and goes to rank tile_target_i // 12; -1 means the tile is dropped; no slot is named twice; at most 2 tiles of one rank go to one rank, and some pair of ranks reaches 2; in every draw some rank receives 12 tiles. `tile_owner_tenant`: at most 2 tiles of one rank have tenants whose storage rows belong to one owner rank, and some rank reaches 2. `tenant_storage_row`: a permutation; storage row p belongs to rank p // 2 of dp.
All inputs are finite; a program needn't handle non-finite values.
Results may differ from the reference program's by a relative error of at most 0.0051.
Values may be sent and summed in bfloat16 or wider, within the bound.
A program may use at most 128 MiB of HBM per device.

```python
import jax
import jax.numpy as jnp
from jax import lax

INPUT_FEATURES = 4096
VALUE_FEATURES = 1024
ADAPTER_RANKS = 32
ROWS = 128
TILE_DEV = 12
TEN_DEV = 2
CAP = 12
TILES = 96
TENANT_COUNT = 16
SLOTS = 96
N_DP = 8


def shared_tenants(key):
    place = jax.random.permutation(jax.random.fold_in(key, 101), TENANT_COUNT).astype(jnp.int32)
    base = jax.random.permutation(jax.random.fold_in(key, 102), N_DP).astype(jnp.int32)
    offset = jax.random.permutation(jax.random.fold_in(key, 103), N_DP).astype(jnp.int32)
    first = jax.random.randint(jax.random.fold_in(key, 104), (TILES,), 0, TEN_DEV).astype(jnp.int32)
    second = jax.random.randint(jax.random.fold_in(key, 105), (TILES,), 0, TEN_DEV).astype(jnp.int32)
    local_row = jnp.minimum(first, second)
    tile_ids = jnp.arange(TILES, dtype=jnp.int32)
    owner = (base[tile_ids // TILE_DEV] + offset[tile_ids % TILE_DEV % N_DP]) % N_DP
    inverse = jnp.argsort(place).astype(jnp.int32)
    tenant = inverse[owner * TEN_DEV + local_row].astype(jnp.int32)
    return (place, tenant)


def draw_tile_owner_tenant(key, part):
    place, tenant = shared_tenants(key)
    return tenant


def draw_tenant_storage_row(key, part):
    place, tenant = shared_tenants(key)
    return place


def draw_tile_slot_target(key, part):
    key = jax.random.fold_in(key, 11)
    key_base, key_shift, key_pos, key_keep, key_full = jax.random.split(key, 5)
    base = jax.random.permutation(key_base, N_DP).astype(jnp.int32)
    shift = jax.random.permutation(key_shift, N_DP).astype(jnp.int32)
    position = jax.random.permutation(key_pos, TILE_DEV).astype(jnp.int32)
    tile_ids = jnp.arange(TILES, dtype=jnp.int32)
    target_rank = (base[tile_ids // TILE_DEV] + shift[tile_ids % TILE_DEV % N_DP]) % N_DP
    slot = target_rank * CAP + position[tile_ids % TILE_DEV]
    full_rank = jax.random.randint(key_full, (), 0, N_DP).astype(jnp.int32)
    kept_tiles = (jax.random.randint(key_keep, (TILES,), 0, 32) != 0) | (target_rank == full_rank)
    return jnp.where(kept_tiles, slot, -1).astype(jnp.int32)


def block_levels(own_key, extent, cuts, least, top_value):
    gain, own = 1.0, jax.random.fold_in(own_key, 6)
    for axis_at, blocks in cuts:
        steps = jnp.exp(jax.random.uniform(jax.random.fold_in(own, axis_at), (blocks,), jnp.float32, least / len(cuts), top_value / len(cuts)))
        gain = gain * jnp.repeat(steps, extent[axis_at] // blocks).reshape([-1 if axis == axis_at else 1 for axis in range(len(extent))])
    return gain


def centred(stream_key, shape, width, reach, shards=(), held_as=jnp.bfloat16):
    gain = block_levels(stream_key, shape, shards, -0.22, 0.18) if shards else 1.0
    entries = jax.random.normal(stream_key, shape, jnp.float32) * width * gain
    return jnp.minimum(jnp.maximum(entries, -reach), reach).astype(held_as)


def setup_inputs(seed: int = 0, part: int = 0) -> dict:
    key_of = jax.random.split(jax.random.key(seed), 9)
    own_keys = jax.random.split(jax.random.fold_in(key_of[8], part), 9)
    input_tiles = centred(own_keys[0], (TILES * ROWS, INPUT_FEATURES), 1.0, 6.0, ((0, 8), (1, 2)))
    value_matrix = centred(key_of[1], (INPUT_FEATURES, VALUE_FEATURES), INPUT_FEATURES ** -0.5, 0.09375, ((0, 2), (1, 8)))
    adapter_down_weight = centred(own_keys[2], (TENANT_COUNT, INPUT_FEATURES, ADAPTER_RANKS), INPUT_FEATURES ** -0.5, 0.09375, ((0, 8), (1, 2)))
    adapter_up_weight = centred(own_keys[3], (TENANT_COUNT, ADAPTER_RANKS, VALUE_FEATURES), ADAPTER_RANKS ** -0.5, 1.0, ((0, 8), (2, 2)))
    output_gradient = centred(own_keys[4], (SLOTS * ROWS, VALUE_FEATURES), 0.5, 3.0, ((0, 8), (1, 2)))
    tile_slot_target = draw_tile_slot_target(jax.random.fold_in(jax.random.fold_in(key_of[8], part), 71), part)
    tile_owner_tenant = draw_tile_owner_tenant(jax.random.fold_in(jax.random.fold_in(key_of[8], part), 71), part)
    tenant_storage_row = draw_tenant_storage_row(jax.random.fold_in(jax.random.fold_in(key_of[8], part), 71), part)
    return {"input_tiles": input_tiles, "value_matrix": value_matrix, "adapter_down_weight": adapter_down_weight, "adapter_up_weight": adapter_up_weight, "output_gradient": output_gradient, "tile_slot_target": tile_slot_target, "tile_owner_tenant": tile_owner_tenant, "tenant_storage_row": tenant_storage_row}


adapter_scale = 0.25


def reference(input_tiles, value_matrix, adapter_down_weight, adapter_up_weight, output_gradient, tile_slot_target, tile_owner_tenant, tenant_storage_row):
    storage_rows = tenant_storage_row[tile_owner_tenant].astype(jnp.int32)
    survives = tile_slot_target >= 0
    safe_slot = jnp.clip(tile_slot_target, 0, SLOTS - 1).astype(jnp.int32)
    grad_slots = output_gradient.reshape(SLOTS, ROWS, VALUE_FEATURES)

    def one_tile(tile_number):
        tile_x = lax.dynamic_slice_in_dim(input_tiles, tile_number * ROWS, ROWS, 0)
        down_matrix = adapter_down_weight[storage_rows[tile_number]]
        up_matrix = adapter_up_weight[storage_rows[tile_number]]
        projected_rows = jnp.dot(tile_x, value_matrix, preferred_element_type=jnp.float32)
        reduced_activation = jnp.dot(tile_x, down_matrix, preferred_element_type=jnp.float32).astype(jnp.bfloat16)
        output_rows = (projected_rows + adapter_scale * jnp.dot(reduced_activation, up_matrix, preferred_element_type=jnp.float32)).astype(jnp.bfloat16)
        tile_gradient = jnp.where(survives[tile_number], grad_slots[safe_slot[tile_number]], jnp.zeros((), jnp.bfloat16))
        reduced_gradient = (adapter_scale * jnp.dot(tile_gradient, up_matrix.T, preferred_element_type=jnp.float32)).astype(jnp.bfloat16)
        a_term = jnp.dot(tile_x.T, reduced_gradient, preferred_element_type=jnp.float32).astype(jnp.bfloat16)
        up_product = (adapter_scale * jnp.dot(reduced_activation.T, tile_gradient, preferred_element_type=jnp.float32)).astype(jnp.bfloat16)
        return output_rows, a_term, up_product

    outputs, a_terms, b_terms = lax.map(one_tile, jnp.arange(TILES, dtype=jnp.int32))
    slot_index = jnp.where(survives, tile_slot_target, SLOTS).astype(jnp.int32)
    moved_out = jnp.zeros((SLOTS, ROWS, VALUE_FEATURES), jnp.bfloat16).at[slot_index].set(outputs, mode="drop")
    grad_a = jnp.zeros((TENANT_COUNT, INPUT_FEATURES, ADAPTER_RANKS), jnp.float32).at[storage_rows].add(a_terms.astype(jnp.float32))
    grad_b = jnp.zeros((TENANT_COUNT, ADAPTER_RANKS, VALUE_FEATURES), jnp.float32).at[storage_rows].add(b_terms.astype(jnp.float32))
    return moved_out.reshape(SLOTS * ROWS, VALUE_FEATURES), grad_a, grad_b
```

```python
import jax
import jax.numpy as jnp
from jax import lax
from jax.sharding import PartitionSpec as P

ROWS = 128
SCALE = 0.25
F32 = jnp.float32
BF16 = jnp.bfloat16


def levels_of(labels, count):
    per_rank = labels.shape[1]
    positions = jnp.arange(per_rank, dtype=jnp.int32)
    earlier = positions[:, None] < positions[None, :]
    same = labels[:, :, None] == labels[:, None, :]
    found = jnp.sum((same & earlier[None]).astype(jnp.int32), axis=1)
    return jnp.minimum(found, count - 1)


def on_device(x, w, a, b, dy, target, tenant, storage):
    ranks = lax.axis_size("dp")
    me = lax.axis_index("dp")
    half = lax.axis_index("mp")
    tiles = x.shape[0] // ROWS
    slots = dy.shape[0] // ROWS
    owned, depth, rank = a.shape
    cols = dy.shape[1]
    places = owned * ranks
    level_count = (tiles + ranks - 1) // ranks

    packed = jnp.concatenate([a.transpose(0, 2, 1), b], axis=2).reshape(owned * rank, depth + cols)
    packed = lax.all_gather(packed, "dp", axis=0, tiled=True)
    w_all = lax.all_gather(w, "dp", axis=0)
    a_all = packed[:, :depth].reshape(places, rank, depth)
    b_all = packed[:, depth:]

    place = storage[tenant].reshape(ranks, tiles)
    goal = target.reshape(ranks, tiles)
    dest = jnp.where(goal >= 0, goal // slots, -1)
    level = levels_of(dest, level_count)
    my_place, my_dest, my_level = place[me], dest[me], level[me]
    slot_ids = me * slots + jnp.arange(slots, dtype=jnp.int32)
    hit = goal.reshape(-1)[None, :] == slot_ids[:, None]
    filled = jnp.any(hit, axis=1)
    source = jnp.argmax(hit, axis=1).astype(jnp.int32)
    slot_src, slot_level = source // tiles, level.reshape(-1)[source]
    slot_place = place.reshape(-1)[source]
    lanes = jnp.arange(ranks * level_count, dtype=jnp.int32)
    tile_lane = jnp.where(my_dest >= 0, my_dest * level_count + my_level, -1)
    slot_lane = jnp.where(filled, slot_src * level_count + slot_level, -1)
    lane_tile = jnp.argmax(tile_lane[None, :] == lanes[:, None], axis=1)
    lane_slot = jnp.argmax(slot_lane[None, :] == lanes[:, None], axis=1)

    xt = x.reshape(tiles, ROWS, depth)
    dyt = dy.reshape(slots, ROWS, cols)
    low_part = jnp.einsum("tqd,tbd->tqb", a_all[my_place], xt, preferred_element_type=F32)
    grad_part = jnp.einsum(
        "sqk,sbk->sqb",
        b_all.reshape(places, rank, cols)[slot_place],
        dyt,
        preferred_element_type=F32,
    )
    both = lax.psum(jnp.concatenate([low_part, grad_part], axis=0), "mp")
    low = both[:tiles].astype(BF16)
    low_grad = (SCALE * both[tiles:]).astype(BF16)
    sent = jnp.concatenate(
        [
            low[lane_tile].reshape(ranks, level_count, rank, ROWS),
            low_grad[lane_slot].reshape(ranks, level_count, rank, ROWS),
        ],
        axis=1,
    )
    got = lax.all_to_all(sent, "dp", split_axis=0, concat_axis=0, tiled=True)
    slot_low = got[:, :level_count].reshape(-1, rank, ROWS)[jnp.maximum(slot_lane, 0)]
    tile_grad = got[:, level_count:].reshape(-1, rank, ROWS)[jnp.maximum(tile_lane, 0)]

    def spread(values, where, keep):
        on = (where[None, :] == jnp.arange(places, dtype=jnp.int32)[:, None]) & keep[None, :]
        full = jnp.where(
            on[:, None, :, None], values.transpose(1, 0, 2)[None], jnp.zeros((), values.dtype)
        )
        return full.reshape(places * rank, -1)

    here = my_dest >= 0
    a_sum = jnp.dot(spread(tile_grad, my_place, here), x, preferred_element_type=F32)
    b_sum = SCALE * jnp.dot(spread(slot_low, slot_place, filled), dy, preferred_element_type=F32)
    sums = jnp.concatenate([a_sum.astype(BF16), b_sum.astype(BF16)], axis=1)
    sums = lax.psum_scatter(sums, "dp", scatter_dimension=0, tiled=True).astype(F32)
    grad_a = sums[:, :depth].reshape(owned, rank, depth).transpose(0, 2, 1)
    grad_b = sums[:, depth:].reshape(owned, rank, cols)

    def project(which):
        part = lax.dynamic_slice_in_dim(w_all, which * (ranks // 2), ranks // 2, 0)
        part = part.transpose(1, 0, 2).reshape(depth, cols)
        return jnp.dot(x, part, preferred_element_type=F32)

    other = lax.ppermute(project(1 - half).astype(BF16), "mp", [(0, 1), (1, 0)])
    low_wide = spread(low, my_place, jnp.ones((tiles,), bool))
    adapted = lax.dot_general(
        low_wide, b_all, (((0,), (0,)), ((), ())), preferred_element_type=F32
    )
    y = (project(half) + SCALE * adapted + other.astype(F32)).astype(BF16)
    y = y.reshape(tiles, ROWS, cols)[lane_tile].reshape(ranks, level_count, ROWS, cols)
    y = lax.all_to_all(y, "dp", split_axis=0, concat_axis=0, tiled=True)
    moved = y.reshape(-1, ROWS, cols)[jnp.maximum(slot_lane, 0)]
    moved = jnp.where(filled[:, None, None], moved, jnp.zeros((), BF16))
    return moved.reshape(slots * ROWS, cols), grad_a, grad_b


def solution(mesh):
    return jax.shard_map(
        on_device,
        mesh=mesh,
        in_specs=(
            P(("group", "dp"), "mp"),
            P("mp", "dp"),
            P(("group", "dp"), "mp", None),
            P(("group", "dp"), None, "mp"),
            P(("group", "dp"), "mp"),
            P("group"),
            P("group"),
            P("group"),
        ),
        out_specs=(
            P(("group", "dp"), "mp"),
            P(("group", "dp"), "mp", None),
            P(("group", "dp"), None, "mp"),
        ),
        check_vma=False,
    )
```

```python
import jax
import jax.numpy as jnp
from jax import lax
from jax.experimental import pallas as pl
from jax.experimental.pallas import tpu as pltpu
from jax.sharding import PartitionSpec as P

ROWS = 128
SCALE = 0.25
F32 = jnp.float32
BF16 = jnp.bfloat16


def levels_of(labels, count):
    per_rank = labels.shape[1]
    positions = jnp.arange(per_rank, dtype=jnp.int32)
    earlier = positions[:, None] < positions[None, :]
    same = labels[:, :, None] == labels[:, None, :]
    found = jnp.sum((same & earlier[None]).astype(jnp.int32), axis=1)
    return jnp.minimum(found, count - 1)


def on_device(x, w, a, b, dy, target, tenant, storage):
    ranks = lax.axis_size("dp")
    me = lax.axis_index("dp")
    half = lax.axis_index("mp")
    tiles = x.shape[0] // ROWS
    slots = dy.shape[0] // ROWS
    owned, depth, rank = a.shape
    cols = dy.shape[1]
    places = owned * ranks
    level_count = (tiles + ranks - 1) // ranks

    packed = jnp.concatenate([a.transpose(0, 2, 1), b], axis=2).reshape(owned * rank, depth + cols)
    packed = lax.all_gather(packed, "dp", axis=0, tiled=True)
    w_all = lax.all_gather(w, "dp", axis=0)
    a_all = packed[:, :depth].reshape(places, rank, depth)
    b_all = packed[:, depth:]

    place = storage[tenant].reshape(ranks, tiles)
    goal = target.reshape(ranks, tiles)
    dest = jnp.where(goal >= 0, goal // slots, -1)
    level = levels_of(dest, level_count)
    my_place, my_dest, my_level = place[me], dest[me], level[me]
    slot_ids = me * slots + jnp.arange(slots, dtype=jnp.int32)
    hit = goal.reshape(-1)[None, :] == slot_ids[:, None]
    filled = jnp.any(hit, axis=1)
    source = jnp.argmax(hit, axis=1).astype(jnp.int32)
    slot_src, slot_level = source // tiles, level.reshape(-1)[source]
    slot_place = place.reshape(-1)[source]
    lanes = jnp.arange(ranks * level_count, dtype=jnp.int32)
    tile_lane = jnp.where(my_dest >= 0, my_dest * level_count + my_level, -1)
    slot_lane = jnp.where(filled, slot_src * level_count + slot_level, -1)
    lane_tile = jnp.argmax(tile_lane[None, :] == lanes[:, None], axis=1)
    lane_slot = jnp.argmax(slot_lane[None, :] == lanes[:, None], axis=1)

    xt = x.reshape(tiles, ROWS, depth)
    dyt = dy.reshape(slots, ROWS, cols)
    low_part = jnp.einsum("tqd,tbd->tqb", a_all[my_place], xt, preferred_element_type=F32)
    grad_part = jnp.einsum(
        "sqk,sbk->sqb",
        b_all.reshape(places, rank, cols)[slot_place],
        dyt,
        preferred_element_type=F32,
    )
    both = lax.psum(jnp.concatenate([low_part, grad_part], axis=0), "mp")
    low = both[:tiles].astype(BF16)
    low_grad = (SCALE * both[tiles:]).astype(BF16)
    sent = jnp.concatenate(
        [
            low[lane_tile].reshape(ranks, level_count, rank, ROWS),
            low_grad[lane_slot].reshape(ranks, level_count, rank, ROWS),
        ],
        axis=1,
    )
    got = lax.all_to_all(sent, "dp", split_axis=0, concat_axis=0, tiled=True)
    slot_low = got[:, :level_count].reshape(-1, rank, ROWS)[jnp.maximum(slot_lane, 0)]
    tile_grad = got[:, level_count:].reshape(-1, rank, ROWS)[jnp.maximum(tile_lane, 0)]

    def spread(values, where, keep):
        on = (where[None, :] == jnp.arange(places, dtype=jnp.int32)[:, None]) & keep[None, :]
        full = jnp.where(
            on[:, None, :, None], values.transpose(1, 0, 2)[None], jnp.zeros((), values.dtype)
        )
        return full.reshape(places * rank, -1)

    here = my_dest >= 0
    a_sum = jnp.dot(spread(tile_grad, my_place, here), x, preferred_element_type=F32)
    b_sum = SCALE * jnp.dot(spread(slot_low, slot_place, filled), dy, preferred_element_type=F32)
    sums = jnp.concatenate([a_sum.astype(BF16), b_sum.astype(BF16)], axis=1)
    sums = lax.psum_scatter(sums, "dp", scatter_dimension=0, tiled=True).astype(F32)
    grad_a = sums[:, :depth].reshape(owned, rank, depth).transpose(0, 2, 1)
    grad_b = sums[:, depth:].reshape(owned, rank, cols)

    def project(which):
        part = lax.dynamic_slice_in_dim(w_all, which * (ranks // 2), ranks // 2, 0)
        part = part.transpose(1, 0, 2).reshape(depth, cols)
        return jnp.dot(x, part, preferred_element_type=F32)

    other = lax.ppermute(project(1 - half).astype(BF16), "mp", [(0, 1), (1, 0)])
    low_wide = spread(low, my_place, jnp.ones((tiles,), bool))
    adapted = lax.dot_general(
        low_wide, b_all, (((0,), (0,)), ((), ())), preferred_element_type=F32
    )
    y = (project(half) + SCALE * adapted + other.astype(F32)).astype(BF16)
    y = y.reshape(tiles, ROWS, cols)[lane_tile].reshape(ranks, level_count, ROWS, cols)
    y = lax.all_to_all(y, "dp", split_axis=0, concat_axis=0, tiled=True)
    moved = y.reshape(-1, ROWS, cols)[jnp.maximum(slot_lane, 0)]
    moved = jnp.where(filled[:, None, None], moved, jnp.zeros((), BF16))
    return moved.reshape(slots * ROWS, cols), grad_a, grad_b

MESH = pl.DeviceIdType.MESH
NT = (((1,), (1,)), ((), ()))


def rank_at(pos):
    pos = lax.rem(pos + 16, 8)
    return jnp.where(pos < 4, 2 * pos, 15 - 2 * pos)


def kernel(
    tab, x, w, ab, dy,
    moved, grads,
    w_all, ab_all, wide, acc, part, part_got, low, grad, swap, swap_got,
    rs_send, rs_got, half_send, half_got, y, y_send, y_got,
    own_sem, ab_sem, w_sem, part_sem, swap_sem, rs_sem, half_sem, y_sem,
):
    tiles, _, depth = x.shape
    cols = dy.shape[2]
    wcols = w.shape[1]
    me = lax.axis_index("dp")
    core = lax.axis_index("mp")
    z, side = me // 2, me % 2
    pos = jnp.where(side == 0, z, 7 - z)
    hops = (rank_at(pos + 1), rank_at(pos - 1))
    o_place, o_got, o_here, o_splace, o_slow, o_sy, o_fill = (tiles * i for i in range(7))
    o_ltile = 7 * tiles
    o_lslot = o_ltile + 16
    zero = jnp.zeros((), BF16)

    def send(source, target, sems, index, device):
        copy = pltpu.make_async_remote_copy(
            src_ref=source, dst_ref=target,
            send_sem=sems.at[(0,) + index], recv_sem=sems.at[(1,) + index],
            device_id=device, device_id_type=MESH,
        )
        copy.start()
        return copy

    own_ab = pltpu.make_async_copy(ab, ab_all.at[pl.ds(2 * me, 2)], own_sem.at[0])
    own_w = pltpu.make_async_copy(
        w, w_all.at[:, pl.ds(pl.multiple_of(me * wcols, wcols), wcols)], own_sem.at[1]
    )
    own_ab.start()
    own_w.start()

    barrier = pltpu.get_barrier_semaphore()
    for d in range(1, 8):
        pl.semaphore_signal(
            barrier, inc=1, device_id={"dp": lax.rem(me + d, 8)}, device_id_type=MESH
        )
    pl.semaphore_signal(barrier, inc=1, device_id={"mp": 1 - core}, device_id_type=MESH)
    pl.semaphore_wait(barrier, 8)

    def ab_step(s):
        out = []
        for way in range(2):
            owner = rank_at(pos - s if way == 0 else pos + s)
            where = ab_all.at[2 * owner + way]
            out.append(send(ab.at[way] if s == 0 else where, where, ab_sem, (way, s),
                            {"dp": hops[way]}))
        return out

    def w_step(s):
        out = []
        rows = depth // 2
        for way in range(2):
            owner = rank_at(pos - s if way == 0 else pos + s)
            there = pl.ds(pl.multiple_of(owner * wcols, wcols), wcols)
            where = w_all.at[pl.ds(way * rows, rows), there]
            out.append(send(w.at[pl.ds(way * rows, rows)] if s == 0 else where, where,
                            w_sem, (way, s), {"dp": hops[way]}))
        return out

    flying = []
    for s in range(7):
        now = ab_step(s)
        flying += now
        for copy in now:
            copy.wait_recv()
    own_ab.wait()

    def low_tiles(first, count):
        def body(i, _):
            t = first + i
            a_t = ab_all[tab[o_place + t]][:, :depth]
            part[t] = lax.dot_general(a_t, x[t], NT, preferred_element_type=F32)
            return 0
        lax.fori_loop(0, count, body, 0)

    def grad_slots():
        def body(s, _):
            b_s = ab_all[tab[o_splace + s]][:, depth:]
            part[tiles + s] = lax.dot_general(b_s, dy[s], NT, preferred_element_type=F32)
            return 0
        lax.fori_loop(0, tiles, body, 0)

    now = w_step(0)
    flying += now
    low_tiles(0, tiles)
    for copy in now:
        copy.wait_recv()

    now = w_step(1)
    flying += now
    grad_slots()
    part_copy = send(part, part_got, part_sem, (), {"mp": 1 - core})
    for copy in now:
        copy.wait_recv()

    now = w_step(2)
    flying += now
    part_copy.wait()

    def settle(t, _):
        low[t] = (part[t] + part_got[t]).astype(BF16)
        grad[t] = (SCALE * (part[tiles + t] + part_got[tiles + t])).astype(BF16)
        return 0
    lax.fori_loop(0, tiles, settle, 0)

    def fill(r, _):
        for l in range(2):
            swap[4 * r + l] = low[tab[o_ltile + 2 * r + l]]
            swap[4 * r + 2 + l] = grad[tab[o_lslot + 2 * r + l]]
        return 0
    lax.fori_loop(0, 8, fill, 0)
    swaps = []
    for d in range(1, 8):
        to = lax.rem(me + d, 8)
        swaps.append(send(swap.at[pl.ds(4 * to, 4)], swap_got.at[pl.ds(4 * me, 4)],
                          swap_sem, (d,), {"dp": to}))
    swap_got[pl.ds(4 * me, 4)] = swap[pl.ds(4 * me, 4)]
    for copy in now:
        copy.wait_recv()

    now = w_step(3)
    flying += now
    for copy in swaps:
        copy.wait()

    def spread(index, keep, place):
        for t in range(tiles):
            value = swap_got[tab[index + t]]
            home = jnp.where(tab[keep + t] > 0, tab[place + t], -1)
            for p in range(16):
                wide[pl.ds(32 * p, 32), pl.ds(ROWS * t, ROWS)] = jnp.where(home == p, value, zero)

    spread(o_got, o_here, o_place)
    for copy in now:
        copy.wait_recv()

    now = w_step(4)
    flying += now

    def a_sum(c, _):
        at = pl.ds(pl.multiple_of(c * 512, 512), 512)
        xs = x[:, :, at].reshape(tiles * ROWS, 512)
        acc[:, :, at] = jnp.dot(wide[...], xs, preferred_element_type=F32).reshape(16, 32, 512)
        return 0
    lax.fori_loop(0, depth // 512, a_sum, 0)
    for copy in now:
        copy.wait_recv()

    now = w_step(5)
    flying += now
    spread(o_slow, o_fill, o_splace)
    acc[:, :, depth:] = SCALE * jnp.dot(
        wide[...], dy[...].reshape(tiles * ROWS, cols), preferred_element_type=F32
    ).reshape(16, 32, cols)
    for copy in now:
        copy.wait_recv()

    now = w_step(6)
    flying += now
    for way in range(2):
        owner = rank_at(pos - 1 if way == 0 else pos + 1)
        rs_send[way, 0] = acc[2 * owner + way].astype(BF16)
    for copy in now:
        copy.wait_recv()
    own_w.wait()

    mine = pl.ds(pl.multiple_of(core * cols, cols), cols)
    theirs = pl.ds(pl.multiple_of((1 - core) * cols, cols), cols)
    halves = []

    def project(k):
        rows = x[pl.ds(2 * k, 2)].reshape(2 * ROWS, depth)
        away = jnp.dot(rows, w_all[:, theirs], preferred_element_type=F32)
        half_send[pl.ds(2 * k, 2)] = away.astype(BF16).reshape(2, ROWS, cols)
        halves.append(send(half_send.at[pl.ds(2 * k, 2)], half_got.at[pl.ds(2 * k, 2)],
                           half_sem, (k,), {"mp": 1 - core}))
        home = jnp.dot(rows, w_all[:, mine], preferred_element_type=F32)
        y[pl.ds(2 * k, 2)] = home.reshape(2, ROWS, cols)

    pieces = tiles // 2
    for s in range(7):
        now = [send(rs_send.at[way, s], rs_got.at[way, s], rs_sem, (way, s), {"dp": hops[way]})
               for way in range(2)]
        flying += now
        if s < pieces:
            project(s)
        for way in range(2):
            now[way].wait_recv()
            if s < 6:
                owner = rank_at(pos - 2 - s if way == 0 else pos + 2 + s)
                rs_send[way, s + 1] = (
                    acc[2 * owner + way] + rs_got[way, s].astype(F32)
                ).astype(BF16)
            else:
                grads[way] = acc[2 * me + way] + rs_got[way, s].astype(F32)

    for copy in halves:
        copy.wait()

    def finish(t, _):
        low_t = jnp.transpose(low[t].astype(F32)).astype(BF16)
        b_t = ab_all[tab[o_place + t]][:, depth:]
        adapted = jnp.dot(low_t, b_t, preferred_element_type=F32)
        total = y[t] + SCALE * adapted + half_got[t].astype(F32)
        half_send[t] = total.astype(BF16)
        return 0
    lax.fori_loop(0, tiles, finish, 0)

    rows_out = []
    for d in range(1, 8):
        to = lax.rem(me + d, 8)
        for l in range(2):
            y_send[2 * to + l] = half_send[tab[o_ltile + 2 * to + l]]
        rows_out.append(send(y_send.at[pl.ds(2 * to, 2)], y_got.at[pl.ds(2 * me, 2)],
                             y_sem, (d,), {"dp": to}))
    for l in range(2):
        y_got[2 * me + l] = half_send[tab[o_ltile + 2 * me + l]]
    for copy in flying:
        copy.wait_send()
    for copy in rows_out:
        copy.wait()

    def place_slot(s, _):
        moved[s] = jnp.where(tab[o_fill + s] > 0, y_got[tab[o_sy + s]], zero)
        return 0
    lax.fori_loop(0, tiles, place_slot, 0)


def pick(mask, values):
    return jnp.sum(jnp.where(mask, values, 0), axis=-1)


def on_grid(x, w, a, b, dy, target, tenant, storage):
    ranks = lax.axis_size("dp")
    me = lax.axis_index("dp")
    tiles = x.shape[0] // ROWS
    owned, depth, rank = a.shape
    cols = dy.shape[1]
    ids = jnp.arange(tenant.shape[0], dtype=jnp.int32)
    place = pick(tenant[:, None] == jnp.arange(storage.shape[0])[None, :], storage[None, :])
    dest = jnp.where(target >= 0, target // tiles, -1)
    rank_of = ids // tiles
    before = (
        (rank_of[:, None] == rank_of[None, :])
        & (dest[:, None] == dest[None, :])
        & (ids[None, :] < ids[:, None])
    )
    level = jnp.minimum(jnp.sum(before.astype(jnp.int32), axis=1), 1)
    mine = me * tiles + jnp.arange(tiles, dtype=jnp.int32)
    at_mine = mine[:, None] == ids[None, :]
    my_place = pick(at_mine, place[None, :])
    my_dest = pick(at_mine, dest[None, :])
    my_level = pick(at_mine, level[None, :])
    here = (my_dest >= 0).astype(jnp.int32)
    my_got = jnp.where(my_dest >= 0, 4 * my_dest + 2 + my_level, 0)
    hit = target[None, :] == mine[:, None]
    filled = jnp.sum(hit.astype(jnp.int32), axis=1)
    s_place = pick(hit, place[None, :])
    s_low = pick(hit, (4 * rank_of + level)[None, :])
    s_row = pick(hit, (2 * rank_of + level)[None, :])
    lanes = jnp.arange(2 * ranks, dtype=jnp.int32)
    order = jnp.arange(tiles, dtype=jnp.int32)
    t_lane = jnp.where(my_dest >= 0, 2 * my_dest + my_level, -1)
    s_lane = jnp.where(filled > 0, s_row, -1)
    lane_tile = pick(lanes[:, None] == t_lane[None, :], order[None, :])
    lane_slot = pick(lanes[:, None] == s_lane[None, :], order[None, :])
    table = jnp.concatenate(
        [my_place, my_got, here, s_place, s_low, s_row, filled, lane_tile, lane_slot]
    ).astype(jnp.int32)
    ab = jnp.concatenate([a.transpose(0, 2, 1), b], axis=2)
    wide = depth + cols
    vmem = pl.BlockSpec(memory_space=pltpu.VMEM)
    dma = pltpu.SemaphoreType.DMA
    tile = (tiles, ROWS, cols)
    moved, grads = pl.pallas_call(
        kernel,
        out_shape=(
            jax.ShapeDtypeStruct(tile, BF16),
            jax.ShapeDtypeStruct((owned, rank, wide), F32),
        ),
        in_specs=[pl.BlockSpec(memory_space=pltpu.SMEM)] + [vmem] * 4,
        out_specs=(vmem, vmem),
        scratch_shapes=[
            pltpu.VMEM((depth, ranks * w.shape[1]), BF16),
            pltpu.VMEM((ranks * owned, rank, wide), BF16),
            pltpu.VMEM((ranks * owned * rank, tiles * ROWS), BF16),
            pltpu.VMEM((ranks * owned, rank, wide), F32),
            pltpu.VMEM((2 * tiles, rank, ROWS), F32),
            pltpu.VMEM((2 * tiles, rank, ROWS), F32),
            pltpu.VMEM((tiles, rank, ROWS), BF16),
            pltpu.VMEM((tiles, rank, ROWS), BF16),
            pltpu.VMEM((4 * ranks, rank, ROWS), BF16),
            pltpu.VMEM((4 * ranks, rank, ROWS), BF16),
            pltpu.VMEM((2, ranks - 1, rank, wide), BF16),
            pltpu.VMEM((2, ranks - 1, rank, wide), BF16),
            pltpu.VMEM(tile, BF16),
            pltpu.VMEM(tile, BF16),
            pltpu.VMEM(tile, F32),
            pltpu.VMEM((2 * ranks, ROWS, cols), BF16),
            pltpu.VMEM((2 * ranks, ROWS, cols), BF16),
            dma((2,)),
            dma((2, 2, ranks - 1)),
            dma((2, 2, ranks - 1)),
            dma((2,)),
            dma((2, ranks)),
            dma((2, 2, ranks - 1)),
            dma((2, tiles // 2)),
            dma((2, ranks)),
        ],
        compiler_params=pltpu.CompilerParams(
            collective_id=0, has_side_effects=True, vmem_limit_bytes=60 * 1024 * 1024
        ),
    )(
        table,
        x.reshape(tiles, ROWS, depth),
        w,
        ab,
        dy.reshape(tiles, ROWS, cols),
    )
    grad_a = grads[:, :, :depth].transpose(0, 2, 1)
    return moved.reshape(tiles * ROWS, cols), grad_a, grads[:, :, depth:]


def solution(mesh):
    return jax.shard_map(
        on_grid if mesh.shape["dp"] == 8 else on_device,
        mesh=mesh,
        in_specs=(
            P(("group", "dp"), "mp"),
            P("mp", "dp"),
            P(("group", "dp"), "mp", None),
            P(("group", "dp"), None, "mp"),
            P(("group", "dp"), "mp"),
            P("group"),
            P("group"),
            P("group"),
        ),
        out_specs=(
            P(("group", "dp"), "mp"),
            P(("group", "dp"), "mp", None),
            P(("group", "dp"), None, "mp"),
        ),
        check_vma=False,
    )
```

```python
import jax
import jax.numpy as jnp
from jax import lax
from jax.experimental import pallas as pl
from jax.experimental.pallas import tpu as pltpu
from jax.sharding import PartitionSpec as P

ROWS = 128
SCALE = 0.25
F32 = jnp.float32
BF16 = jnp.bfloat16


def levels_of(labels, count):
    per_rank = labels.shape[1]
    positions = jnp.arange(per_rank, dtype=jnp.int32)
    earlier = positions[:, None] < positions[None, :]
    same = labels[:, :, None] == labels[:, None, :]
    found = jnp.sum((same & earlier[None]).astype(jnp.int32), axis=1)
    return jnp.minimum(found, count - 1)


def on_device(x, w, a, b, dy, target, tenant, storage):
    ranks = lax.axis_size("dp")
    me = lax.axis_index("dp")
    half = lax.axis_index("mp")
    tiles = x.shape[0] // ROWS
    slots = dy.shape[0] // ROWS
    owned, depth, rank = a.shape
    cols = dy.shape[1]
    places = owned * ranks
    level_count = (tiles + ranks - 1) // ranks

    packed = jnp.concatenate([a.transpose(0, 2, 1), b], axis=2).reshape(owned * rank, depth + cols)
    packed = lax.all_gather(packed, "dp", axis=0, tiled=True)
    w_all = lax.all_gather(w, "dp", axis=0)
    a_all = packed[:, :depth].reshape(places, rank, depth)
    b_all = packed[:, depth:]

    place = storage[tenant].reshape(ranks, tiles)
    goal = target.reshape(ranks, tiles)
    dest = jnp.where(goal >= 0, goal // slots, -1)
    level = levels_of(dest, level_count)
    my_place, my_dest, my_level = place[me], dest[me], level[me]
    slot_ids = me * slots + jnp.arange(slots, dtype=jnp.int32)
    hit = goal.reshape(-1)[None, :] == slot_ids[:, None]
    filled = jnp.any(hit, axis=1)
    source = jnp.argmax(hit, axis=1).astype(jnp.int32)
    slot_src, slot_level = source // tiles, level.reshape(-1)[source]
    slot_place = place.reshape(-1)[source]
    lanes = jnp.arange(ranks * level_count, dtype=jnp.int32)
    tile_lane = jnp.where(my_dest >= 0, my_dest * level_count + my_level, -1)
    slot_lane = jnp.where(filled, slot_src * level_count + slot_level, -1)
    lane_tile = jnp.argmax(tile_lane[None, :] == lanes[:, None], axis=1)
    lane_slot = jnp.argmax(slot_lane[None, :] == lanes[:, None], axis=1)

    xt = x.reshape(tiles, ROWS, depth)
    dyt = dy.reshape(slots, ROWS, cols)
    low_part = jnp.einsum("tqd,tbd->tqb", a_all[my_place], xt, preferred_element_type=F32)
    grad_part = jnp.einsum(
        "sqk,sbk->sqb",
        b_all.reshape(places, rank, cols)[slot_place],
        dyt,
        preferred_element_type=F32,
    )
    both = lax.psum(jnp.concatenate([low_part, grad_part], axis=0), "mp")
    low = both[:tiles].astype(BF16)
    low_grad = (SCALE * both[tiles:]).astype(BF16)
    sent = jnp.concatenate(
        [
            low[lane_tile].reshape(ranks, level_count, rank, ROWS),
            low_grad[lane_slot].reshape(ranks, level_count, rank, ROWS),
        ],
        axis=1,
    )
    got = lax.all_to_all(sent, "dp", split_axis=0, concat_axis=0, tiled=True)
    slot_low = got[:, :level_count].reshape(-1, rank, ROWS)[jnp.maximum(slot_lane, 0)]
    tile_grad = got[:, level_count:].reshape(-1, rank, ROWS)[jnp.maximum(tile_lane, 0)]

    def spread(values, where, keep):
        on = (where[None, :] == jnp.arange(places, dtype=jnp.int32)[:, None]) & keep[None, :]
        full = jnp.where(
            on[:, None, :, None], values.transpose(1, 0, 2)[None], jnp.zeros((), values.dtype)
        )
        return full.reshape(places * rank, -1)

    here = my_dest >= 0
    a_sum = jnp.dot(spread(tile_grad, my_place, here), x, preferred_element_type=F32)
    b_sum = SCALE * jnp.dot(spread(slot_low, slot_place, filled), dy, preferred_element_type=F32)
    sums = jnp.concatenate([a_sum.astype(BF16), b_sum.astype(BF16)], axis=1)
    sums = lax.psum_scatter(sums, "dp", scatter_dimension=0, tiled=True).astype(F32)
    grad_a = sums[:, :depth].reshape(owned, rank, depth).transpose(0, 2, 1)
    grad_b = sums[:, depth:].reshape(owned, rank, cols)

    def project(which):
        part = lax.dynamic_slice_in_dim(w_all, which * (ranks // 2), ranks // 2, 0)
        part = part.transpose(1, 0, 2).reshape(depth, cols)
        return jnp.dot(x, part, preferred_element_type=F32)

    other = lax.ppermute(project(1 - half).astype(BF16), "mp", [(0, 1), (1, 0)])
    low_wide = spread(low, my_place, jnp.ones((tiles,), bool))
    adapted = lax.dot_general(
        low_wide, b_all, (((0,), (0,)), ((), ())), preferred_element_type=F32
    )
    y = (project(half) + SCALE * adapted + other.astype(F32)).astype(BF16)
    y = y.reshape(tiles, ROWS, cols)[lane_tile].reshape(ranks, level_count, ROWS, cols)
    y = lax.all_to_all(y, "dp", split_axis=0, concat_axis=0, tiled=True)
    moved = y.reshape(-1, ROWS, cols)[jnp.maximum(slot_lane, 0)]
    moved = jnp.where(filled[:, None, None], moved, jnp.zeros((), BF16))
    return moved.reshape(slots * ROWS, cols), grad_a, grad_b

MESH = pl.DeviceIdType.MESH
NT = (((1,), (1,)), ((), ()))


def rank_at(pos):
    pos = lax.rem(pos + 16, 8)
    return jnp.where(pos < 4, 2 * pos, 15 - 2 * pos)


def kernel(
    tab, x, w, a, b, dy,
    moved, grad_a, grad_b,
    w_all, ab_all, wide, acc, part, part_got, low, grad, swap, swap_got,
    rs_send, rs_got, half_send, half_got, y, y_send, y_got,
    own_sem, ab_sem, w_sem, x_sem, part_sem, swap_sem, rs_sem, half_sem, y_sem,
):
    tiles, _, depth = x.shape
    cols = dy.shape[2]
    wcols = w.shape[1]
    me = lax.axis_index("dp")
    core = lax.axis_index("mp")
    group = lax.axis_index("group")
    z, side = me // 2, me % 2
    pos = jnp.where(side == 0, z, 7 - z)
    hops = (rank_at(pos + 1), rank_at(pos - 1))
    o_place, o_got, o_here, o_splace, o_slow, o_sy, o_fill = (tiles * i for i in range(7))
    o_ltile = 7 * tiles
    o_lslot = o_ltile + 16
    zero = jnp.zeros((), BF16)

    def send(source, target, sems, index, device):
        copy = pltpu.make_async_remote_copy(
            src_ref=source, dst_ref=target,
            send_sem=sems.at[(0,) + index], recv_sem=sems.at[(1,) + index],
            device_id=device, device_id_type=MESH,
        )
        copy.start()
        return copy

    own_a = pltpu.make_async_copy(
        a, ab_all.at[pl.ds(2 * me, 2), :, pl.ds(0, depth)], own_sem.at[0]
    )
    own_b = pltpu.make_async_copy(
        b, ab_all.at[pl.ds(2 * me, 2), :, pl.ds(depth, cols)], own_sem.at[2]
    )
    own_w = pltpu.make_async_copy(
        w, w_all.at[:, pl.ds(pl.multiple_of(me * wcols, wcols), wcols)], own_sem.at[1]
    )
    own_a.start()
    own_b.start()
    own_w.start()

    barrier = pltpu.get_barrier_semaphore()
    for d in range(1, 8):
        pl.semaphore_signal(
            barrier, inc=1, device_id={"dp": lax.rem(me + d, 8)}, device_id_type=MESH
        )
    pl.semaphore_signal(barrier, inc=1, device_id={"mp": 1 - core}, device_id_type=MESH)
    pl.semaphore_signal(barrier, inc=1, device_id={"group": 1 - group}, device_id_type=MESH)
    pl.semaphore_wait(barrier, 9)

    def ab_step(s):
        out = []
        for way in range(2):
            owner = rank_at(pos - s if way == 0 else pos + s)
            where = ab_all.at[2 * owner + way]
            out.append(send(where, where, ab_sem, (way, s),
                            {"dp": hops[way]}))
        return out

    ring = depth * 11 // 16
    crossing = depth - ring
    ring_from = pl.multiple_of(jnp.where(group == 0, crossing, 0), 64)
    cross_from = pl.multiple_of(jnp.where(group == 0, ring, 0), 64)

    def column(owner):
        return pl.ds(pl.multiple_of(owner * wcols, wcols), wcols)

    def w_step(s):
        out = []
        rows = ring // 2
        for way in range(2):
            owner = rank_at(pos - s if way == 0 else pos + s)
            here = pl.ds(pl.multiple_of(ring_from + way * rows, 64), rows)
            where = w_all.at[here, column(owner)]
            out.append(send(w.at[here] if s == 0 else where, where,
                            w_sem, (way, s), {"dp": hops[way]}))
        return out

    def w_arrive(s, copies):
        for copy in copies:
            copy.wait_recv()
        owner = rank_at(jnp.where(group == 0, pos + 1 + s, pos - 1 - s))
        where = w_all.at[pl.ds(cross_from, crossing), column(owner)]
        return send(where, where, x_sem, (s,), {"group": 1 - group})

    flying = []
    crossings = []
    own_a.wait()
    own_b.wait()
    w_now = None
    for s in range(7):
        now = ab_step(s)
        flying += now
        if s % 2 == 0 and s < 6:
            if s > 0:
                crossings.append(w_arrive(s // 2 - 1, w_now))
            w_now = w_step(s // 2)
            flying += w_now
        for copy in now:
            copy.wait_recv()

    def w_next(s):
        crossings.append(w_arrive(s - 1, w_now))
        copies = w_step(s)
        flying.extend(copies)
        return copies

    def low_tiles(first, count):
        def body(i, _):
            t = first + i
            a_t = ab_all[tab[o_place + t]][:, :depth]
            part[t] = lax.dot_general(a_t, x[t], NT, preferred_element_type=F32)
            return 0
        lax.fori_loop(0, count, body, 0)

    def grad_slots():
        def body(s, _):
            b_s = ab_all[tab[o_splace + s]][:, depth:]
            part[tiles + s] = lax.dot_general(b_s, dy[s], NT, preferred_element_type=F32)
            return 0
        lax.fori_loop(0, tiles, body, 0)

    low_tiles(0, tiles // 2)
    w_now = w_next(3)
    low_tiles(tiles // 2, tiles - tiles // 2)
    grad_slots()
    part_copy = send(part, part_got, part_sem, (), {"mp": 1 - core})
    w_now = w_next(4)
    part_copy.wait()

    def settle(t, _):
        low[t] = (part[t] + part_got[t]).astype(BF16)
        grad[t] = (SCALE * (part[tiles + t] + part_got[tiles + t])).astype(BF16)
        return 0
    lax.fori_loop(0, tiles, settle, 0)

    def fill(r, _):
        for l in range(2):
            swap[4 * r + l] = low[tab[o_ltile + 2 * r + l]]
            swap[4 * r + 2 + l] = grad[tab[o_lslot + 2 * r + l]]
        return 0
    lax.fori_loop(0, 8, fill, 0)
    swaps = []
    for d in range(1, 8):
        to = lax.rem(me + d, 8)
        swaps.append(send(swap.at[pl.ds(4 * to, 4)], swap_got.at[pl.ds(4 * me, 4)],
                          swap_sem, (d,), {"dp": to}))
    swap_got[pl.ds(4 * me, 4)] = swap[pl.ds(4 * me, 4)]
    for copy in swaps:
        copy.wait()

    def spread(index, keep, place):
        for t in range(tiles):
            value = swap_got[tab[index + t]]
            home = jnp.where(tab[keep + t] > 0, tab[place + t], -1)
            for p in range(16):
                wide[pl.ds(32 * p, 32), pl.ds(ROWS * t, ROWS)] = jnp.where(home == p, value, zero)

    spread(o_got, o_here, o_place)
    w_now = w_next(5)

    def a_sum(c, _):
        at = pl.ds(pl.multiple_of(c * 512, 512), 512)
        xs = x[:, :, at].reshape(tiles * ROWS, 512)
        acc[:, :, at] = jnp.dot(wide[...], xs, preferred_element_type=F32).reshape(16, 32, 512)
        return 0
    lax.fori_loop(0, depth // 512, a_sum, 0)
    w_now = w_next(6)
    spread(o_slow, o_fill, o_splace)
    acc[:, :, depth:] = SCALE * jnp.dot(
        wide[...], dy[...].reshape(tiles * ROWS, cols), preferred_element_type=F32
    ).reshape(16, 32, cols)
    block = (depth + cols) // 2
    rs_now = {}

    def rs_store(s, way, c, value):
        rs_send[way, s, c] = value
        rs_now[s, way, c] = send(rs_send.at[way, s, c], rs_got.at[way, s, c],
                                 rs_sem, (way, s, c), {"dp": hops[way]})
        flying.append(rs_now[s, way, c])

    def rs_advance(s, c):
        at = pl.ds(c * block, block)
        for way in range(2):
            rs_now[s, way, c].wait_recv()
            got = rs_got[way, s, c].astype(F32)
            if s < 6:
                owner = rank_at(pos - 2 - s if way == 0 else pos + 2 + s)
                rs_store(s + 1, way, c, (acc[2 * owner + way, :, at] + got).astype(BF16))
            else:
                total = acc[2 * me + way, :, at] + got
                if c == 0:
                    grad_a[way, :, pl.ds(0, block)] = total
                else:
                    grad_a[way, :, pl.ds(block, depth - block)] = total[:, : depth - block]
                    grad_b[way] = total[:, depth - block :]

    for c in range(2):
        for way in range(2):
            owner = rank_at(pos - 1 if way == 0 else pos + 1)
            rs_store(0, way, c, acc[2 * owner + way, :, pl.ds(c * block, block)].astype(BF16))
    crossings.append(w_arrive(6, w_now))
    own_w.wait()
    rs_advance(0, 0)
    rs_advance(0, 1)
    for copy in crossings:
        copy.wait()

    mine = pl.ds(pl.multiple_of(core * cols, cols), cols)
    theirs = pl.ds(pl.multiple_of((1 - core) * cols, cols), cols)
    halves = []

    def project(k, part_of):
        rows = x[pl.ds(2 * k, 2)].reshape(2 * ROWS, depth)
        if part_of == 0:
            away = jnp.dot(rows, w_all[:, theirs], preferred_element_type=F32)
            half_send[pl.ds(2 * k, 2)] = away.astype(BF16).reshape(2, ROWS, cols)
            halves.append(send(half_send.at[pl.ds(2 * k, 2)], half_got.at[pl.ds(2 * k, 2)],
                               half_sem, (k,), {"mp": 1 - core}))
        else:
            home = jnp.dot(rows, w_all[:, mine], preferred_element_type=F32)
            y[pl.ds(2 * k, 2)] = home.reshape(2, ROWS, cols)

    todo = [(s, c) for s in range(1, 7) for c in range(2)]
    for part_of in range(2):
        for k in range(tiles // 2):
            project(k, part_of)
            if k % 2 == 1:
                rs_advance(*todo.pop(0))

    for copy in halves:
        copy.wait()

    def finish(t, _):
        low_t = jnp.transpose(low[t].astype(F32)).astype(BF16)
        b_t = ab_all[tab[o_place + t]][:, depth:]
        adapted = jnp.dot(low_t, b_t, preferred_element_type=F32)
        total = y[t] + SCALE * adapted + half_got[t].astype(F32)
        half_send[t] = total.astype(BF16)
        return 0
    lax.fori_loop(0, tiles, finish, 0)

    rows_out = []
    for d in range(1, 8):
        to = lax.rem(me + d, 8)
        for l in range(2):
            y_send[2 * to + l] = half_send[tab[o_ltile + 2 * to + l]]
        rows_out.append(send(y_send.at[pl.ds(2 * to, 2)], y_got.at[pl.ds(2 * me, 2)],
                             y_sem, (d,), {"dp": to}))
    for l in range(2):
        y_got[2 * me + l] = half_send[tab[o_ltile + 2 * me + l]]
    for s, c in todo:
        rs_advance(s, c)
    for copy in flying:
        copy.wait_send()
    for copy in rows_out:
        copy.wait()

    def place_slot(s, _):
        moved[s] = jnp.where(tab[o_fill + s] > 0, y_got[tab[o_sy + s]], zero)
        return 0
    lax.fori_loop(0, tiles, place_slot, 0)


def pick(mask, values):
    return jnp.sum(jnp.where(mask, values, 0), axis=-1)


def on_grid(x, w, a, b, dy, target, tenant, storage):
    ranks = lax.axis_size("dp")
    me = lax.axis_index("dp")
    tiles = x.shape[0] // ROWS
    owned, depth, rank = a.shape
    cols = dy.shape[1]
    ids = jnp.arange(tenant.shape[0], dtype=jnp.int32)
    place = pick(tenant[:, None] == jnp.arange(storage.shape[0])[None, :], storage[None, :])
    dest = jnp.where(target >= 0, target // tiles, -1)
    rank_of = ids // tiles
    before = (
        (rank_of[:, None] == rank_of[None, :])
        & (dest[:, None] == dest[None, :])
        & (ids[None, :] < ids[:, None])
    )
    level = jnp.minimum(jnp.sum(before.astype(jnp.int32), axis=1), 1)
    mine = me * tiles + jnp.arange(tiles, dtype=jnp.int32)
    at_mine = mine[:, None] == ids[None, :]
    my_place = pick(at_mine, place[None, :])
    my_dest = pick(at_mine, dest[None, :])
    my_level = pick(at_mine, level[None, :])
    here = (my_dest >= 0).astype(jnp.int32)
    my_got = jnp.where(my_dest >= 0, 4 * my_dest + 2 + my_level, 0)
    hit = target[None, :] == mine[:, None]
    filled = jnp.sum(hit.astype(jnp.int32), axis=1)
    s_place = pick(hit, place[None, :])
    s_low = pick(hit, (4 * rank_of + level)[None, :])
    s_row = pick(hit, (2 * rank_of + level)[None, :])
    lanes = jnp.arange(2 * ranks, dtype=jnp.int32)
    order = jnp.arange(tiles, dtype=jnp.int32)
    t_lane = jnp.where(my_dest >= 0, 2 * my_dest + my_level, -1)
    s_lane = jnp.where(filled > 0, s_row, -1)
    lane_tile = pick(lanes[:, None] == t_lane[None, :], order[None, :])
    lane_slot = pick(lanes[:, None] == s_lane[None, :], order[None, :])
    table = jnp.concatenate(
        [my_place, my_got, here, s_place, s_low, s_row, filled, lane_tile, lane_slot]
    ).astype(jnp.int32)
    wide = depth + cols
    vmem = pl.BlockSpec(memory_space=pltpu.VMEM)
    dma = pltpu.SemaphoreType.DMA
    tile = (tiles, ROWS, cols)
    moved, grad_a, grad_b = pl.pallas_call(
        kernel,
        out_shape=(
            jax.ShapeDtypeStruct(tile, BF16),
            jax.ShapeDtypeStruct((owned, rank, depth), F32),
            jax.ShapeDtypeStruct((owned, rank, cols), F32),
        ),
        in_specs=[pl.BlockSpec(memory_space=pltpu.SMEM)] + [vmem] * 5,
        out_specs=(vmem, vmem, vmem),
        scratch_shapes=[
            pltpu.VMEM((depth, ranks * w.shape[1]), BF16),
            pltpu.VMEM((ranks * owned, rank, wide), BF16),
            pltpu.VMEM((ranks * owned * rank, tiles * ROWS), BF16),
            pltpu.VMEM((ranks * owned, rank, wide), F32),
            pltpu.VMEM((2 * tiles, rank, ROWS), F32),
            pltpu.VMEM((2 * tiles, rank, ROWS), F32),
            pltpu.VMEM((tiles, rank, ROWS), BF16),
            pltpu.VMEM((tiles, rank, ROWS), BF16),
            pltpu.VMEM((4 * ranks, rank, ROWS), BF16),
            pltpu.VMEM((4 * ranks, rank, ROWS), BF16),
            pltpu.VMEM((2, ranks - 1, 2, rank, wide // 2), BF16),
            pltpu.VMEM((2, ranks - 1, 2, rank, wide // 2), BF16),
            pltpu.VMEM(tile, BF16),
            pltpu.VMEM(tile, BF16),
            pltpu.VMEM(tile, F32),
            pltpu.VMEM((2 * ranks, ROWS, cols), BF16),
            pltpu.VMEM((2 * ranks, ROWS, cols), BF16),
            dma((3,)),
            dma((2, 2, ranks - 1)),
            dma((2, 2, ranks - 1)),
            dma((2, ranks - 1)),
            dma((2,)),
            dma((2, ranks)),
            dma((2, 2, ranks - 1, 2)),
            dma((2, tiles // 2)),
            dma((2, ranks)),
        ],
        compiler_params=pltpu.CompilerParams(
            collective_id=0, has_side_effects=True, vmem_limit_bytes=60 * 1024 * 1024
        ),
    )(
        table,
        x.reshape(tiles, ROWS, depth),
        w,
        a.transpose(0, 2, 1),
        b,
        dy.reshape(tiles, ROWS, cols),
    )
    return moved.reshape(tiles * ROWS, cols), grad_a.transpose(0, 2, 1), grad_b


def solution(mesh):
    return jax.shard_map(
        on_grid if (mesh.shape["dp"], mesh.shape["group"]) == (8, 2) else on_device,
        mesh=mesh,
        in_specs=(
            P(("group", "dp"), "mp"),
            P("mp", "dp"),
            P(("group", "dp"), "mp", None),
            P(("group", "dp"), None, "mp"),
            P(("group", "dp"), "mp"),
            P("group"),
            P("group"),
            P("group"),
        ),
        out_specs=(
            P(("group", "dp"), "mp"),
            P(("group", "dp"), "mp", None),
            P(("group", "dp"), None, "mp"),
        ),
        check_vma=False,
    )
```
